32 devices in a mesh: space: 8 (over z, y), mode: 4 (over x, core).
Axes of the slice: x: 2, y: 2, z: 4, core: 2. Of those that a mesh axis runs over, the one named last changes fastest.
Arguments:
- iterate: float32 [84, 16, 6144], P('mode', None, 'space'), may hold values from -6 to 6
- forcing: float32 [84, 16, 6144], P('mode', None, 'space'), may hold values from -6 to 6
- tiles: bfloat16 [3, 32, 3, 36864], P(None, 'space'), may hold values from -0.25 to 0.25
- inverse_blocks: bfloat16 [32, 36864], P('space'), may hold values from -0.4375 to 0.4375
- columns: int32 [32, 3], P('space'), may hold values from 0 to 7, as said below
- coupling: float32 [3, 84, 84], replicated, may hold values from -0.7 to 1.5, as said below
Outputs:
- updated: float32 [84, 16, 6144], P('mode', None, 'space')
- residual: float32 [84, 16, 6144], P('mode', None, 'space')
The draws below stay inside these ranges and needn't reach their ends.
Inputs may be any that keep to these rules, and one draw needn't show every extreme that they name: For row block j at position q = j mod 4 of its device: columns[j, 0] = 2 + q; columns[j, 1] = 2 + q - 1 or 2 + q - 2; columns[j, 2] = 2 + q + 1 or 2 + q + 2. At q = 0 slot 1 is 2 + q - 2, at q = 3 slot 2 is 2 + q + 2. `coupling`: each matrix is symmetric; the first has ones added on its diagonal.
All inputs are finite; a program needn't handle non-finite values.
Results may differ from the reference program's by a relative error of at most 0.0033.
Values may be sent and summed in bfloat16 or wider, within the bound.
A program may use at most 64 MiB of HBM per device.

```python
import jax
import jax.numpy as jnp
from jax import lax

P_SIZE = 84
BS = 192
KL = 3
S = 3
H = 2
B_LOC = 4
LOADS = 16
NB = 32
NDOF = 6144


def draw_columns(key, part):
    position = jnp.arange(NB, dtype=jnp.int32) % B_LOC
    reach = jax.random.randint(key, (NB, 2), 1, 3, dtype=jnp.int32)
    behind = jnp.where(position == 0, 2, reach[:, 0])
    ahead = jnp.where(position == B_LOC - 1, 2, reach[:, 1])
    stacked = jnp.stack([H + position, H + position - behind, H + position + ahead], axis=1)
    return stacked.astype(jnp.int32)


def draw_coupling(key, part):
    first_key, second_key = jax.random.split(key)
    raw_values = jnp.clip(jax.random.normal(first_key, (KL, P_SIZE, P_SIZE), jnp.float32), -4.0, 4.0)
    pattern = jax.random.uniform(second_key, (KL, P_SIZE, P_SIZE), jnp.float32)
    pattern = pattern + jnp.swapaxes(pattern, 1, 2)
    kept = jnp.where(pattern < 0.7, 1.0, 0.0)
    values = (raw_values + jnp.swapaxes(raw_values, 1, 2)) * 0.7071 * kept
    scales = jnp.where(jnp.arange(KL) == 0, 0.08, 0.12)[:, None, None]
    diagonal = jnp.where(jnp.arange(P_SIZE)[:, None] == jnp.arange(P_SIZE)[None, :], 1.0, 0.0)
    first_term = jnp.where(jnp.arange(KL) == 0, 1.0, 0.0)[:, None, None]
    return (values * scales + first_term * diagonal[None]).astype(jnp.float32)


def block_levels(stream_key, extent, pieces, low, high):
    def one(axis_at, shards_of):
        heights = jax.random.uniform(jax.random.fold_in(jax.random.fold_in(stream_key, 6), axis_at), (shards_of,), jnp.float32, low / len(pieces), high / len(pieces))
        return jnp.repeat(jnp.exp(heights), extent[axis_at] // shards_of).reshape((-1,) + (1,) * (len(extent) - axis_at - 1))

    loudness = one(*pieces[0])
    for cut in pieces[1:]:
        loudness = loudness * one(*cut)
    return loudness


def bell_draw(rng, shape, width, most, cuts=(), kind=jnp.bfloat16):
    drawn = jax.random.normal(rng, shape, jnp.float32) * width
    if len(cuts) > 0:
        drawn = block_levels(rng, shape, cuts, -0.22, 0.18) * drawn
    return jnp.clip(drawn, min=-most, max=most).astype(kind)


def setup_inputs(seed: int = 0) -> dict:
    splits = jax.random.split(jax.random.key(seed), 7)
    iterate = bell_draw(splits[0], (P_SIZE, LOADS, NDOF), 1.0, 6.0, ((0, 4), (2, 8)), jnp.float32)
    forcing = bell_draw(splits[1], (P_SIZE, LOADS, NDOF), 1.0, 6.0, ((0, 4), (2, 8)), jnp.float32)
    tiles = bell_draw(splits[2], (KL, NB, S, BS * BS), (S * BS) ** -0.5, 0.25, ((1, 8),))
    inverse_blocks = bell_draw(splits[3], (NB, BS * BS), BS ** -0.5, 0.4375, ((0, 8),))
    columns = draw_columns(jax.random.fold_in(splits[6], 71), 0)
    coupling = draw_coupling(jax.random.fold_in(splits[6], 71), 0)
    return {"iterate": iterate, "forcing": forcing, "tiles": tiles, "inverse_blocks": inverse_blocks, "columns": columns, "coupling": coupling}


RELAXATION = 0.7


def reference(iterate, forcing, tiles, inverse_blocks, columns, coupling):
    rounded = iterate.astype(jnp.bfloat16)
    rounded = lax.optimization_barrier(rounded).astype(jnp.float32).reshape(P_SIZE, LOADS, NB, BS)
    blocks = jnp.arange(NB, dtype=jnp.int32)
    anchor = (blocks // B_LOC) * B_LOC - H
    target = ((anchor[:, None] + columns.astype(jnp.int32)) % NB).astype(jnp.int32)
    picked = rounded[:, :, target, :]

    def one_term(tile_term):
        shaped = tile_term.astype(jnp.float32).reshape(NB, S, BS, BS)
        return jnp.einsum("rsim,plrsm->plri", shaped, picked).astype(jnp.bfloat16)

    products = lax.map(one_term, tiles)
    products = lax.optimization_barrier(products)
    flat = products.astype(jnp.float32).reshape(KL, P_SIZE, LOADS, NB * BS)
    applied = jnp.einsum("kab,kbln->aln", coupling, flat, precision=lax.Precision.HIGHEST)
    residual = forcing - applied
    rounded_res = lax.optimization_barrier(residual.astype(jnp.bfloat16))
    rounded_res = rounded_res.astype(jnp.float32).reshape(P_SIZE, LOADS, NB, BS)
    inverse = inverse_blocks.astype(jnp.float32).reshape(NB, BS, BS)
    update = jnp.einsum("jim,pljm->plji", inverse, rounded_res).reshape(P_SIZE, LOADS, NB * BS)
    updated = iterate + RELAXATION * update
    return updated, residual
```

```python
import functools

import jax
import jax.numpy as jnp
from jax import lax
from jax.experimental import pallas as pl
from jax.experimental.pallas import tpu as pltpu
from jax.sharding import PartitionSpec as P

RELAXATION = 0.7
BF = jnp.bfloat16
F32 = jnp.float32
MESH = pl.DeviceIdType.MESH
ANY = pl.BlockSpec(memory_space=pl.ANY)


def nt(a, b):
    return lax.dot_general(a, b, (((1,), (1,)), ((), ())), preferred_element_type=F32)


def nn(a, b):
    return jnp.dot(a, b, preferred_element_type=F32)


def iota(shape, dim):
    return lax.broadcasted_iota(jnp.int32, shape, dim)


def kernel(
    cfg,
    cols_ref, it_ref, c_ref, fo_hbm, tiles_hbm, inv_hbm,
    upd_ref, res_ref,
    fo_ref, tiles_ref, inv_ref, xe, acc, prod, kron, own, a_out, a_in, b_out, b_in, c_out, c_in,
    lsem, hs, hr, as_, ar, bs, br, cs, cr,
):
    modes, loads, bsz, terms, seg = cfg
    rows = modes * loads
    half = 2 * bsz
    n_space = lax.axis_size("space")
    me_s = lax.axis_index("space")
    me = lax.axis_index("mode")
    right = lax.rem(me_s + 1, n_space)
    left = lax.rem(me_s + n_space - 1, n_space)
    near = me + 1 - 2 * lax.rem(me, 2)
    far = lax.rem(me + 2, 4)
    diag = lax.rem(near + 2, 4)
    to_right, to_left = (right, me), (left, me)
    to_near, to_far = (me_s, near), (me_s, far)

    loads_in = [
        pltpu.make_async_copy(tiles_hbm, tiles_ref, lsem.at[0]),
        pltpu.make_async_copy(fo_hbm, fo_ref, lsem.at[1]),
        pltpu.make_async_copy(inv_hbm, inv_ref, lsem.at[2]),
    ]
    for cp in loads_in:
        cp.start()

    barrier = pltpu.get_barrier_semaphore()
    for who in (to_right, to_left, to_near, to_far):
        pl.semaphore_signal(barrier, inc=1, device_id=who, device_id_type=MESH)
    for h in range(2):
        xe[1 + h] = it_ref[:, h * half : (h + 1) * half].astype(BF)
    pl.semaphore_wait(barrier, 4)

    def remote(src, dst, s, r, who):
        return pltpu.make_async_remote_copy(
            src_ref=src, dst_ref=dst, send_sem=s, recv_sem=r, device_id=who, device_id_type=MESH
        )

    halo = [
        remote(xe.at[2], xe.at[0], hs.at[0], hr.at[0], to_right),
        remote(xe.at[1], xe.at[3], hs.at[1], hr.at[1], to_left),
    ]
    for cp in halo:
        cp.start()

    total = c_ref.shape[1]
    col = iota((total, seg), 1)
    pick = (iota((total, seg), 0) == me * modes + col // loads) & (col < rows)
    pick = jnp.where(pick, 1.0, 0.0).astype(BF)
    spread = [nn(c_ref[k].astype(BF), pick).astype(BF) for k in range(terms)]
    same = (iota((rows, seg), 0) % loads) == (iota((rows, seg), 1) % loads)
    for n, dest in enumerate((diag, far, near, me)):
        e = iota((rows, total), 1) == dest * modes + iota((rows, total), 0) // loads
        e = jnp.where(e, 1.0, 0.0).astype(BF)
        for k in range(terms):
            kron[n, :, k * seg : (k + 1) * seg] = jnp.where(same, nn(e, spread[k]), 0.0).astype(BF)
    for h in range(2):
        for k in range(terms):
            prod[h, k * seg + rows : (k + 1) * seg, :] = jnp.zeros((seg - rows, half), BF)

    def block(q):
        p = q + 2
        return xe[p // 2, :, (p % 2) * bsz : (p % 2 + 1) * bsz]

    loads_in[0].wait()

    def early(q, s):
        near_, far_ = (q - 1, q - 2) if s == 1 else (q + 1, q + 2)
        return jnp.where(cols_ref[q, s] == near_ + 2, block(near_), block(far_))

    for q in range(4):
        s = 2 if q < 2 else 1
        a0, a1 = block(q), early(q, s)
        for k in range(terms):
            acc[k, q] = nt(a0, tiles_ref[k, 0, q]) + nt(a1, tiles_ref[k, s, q])

    for cp in halo:
        cp.wait()

    def late(h):
        for q in (2 * h, 2 * h + 1):
            s = 1 if q < 2 else 2
            if q == 0:
                x = block(-2)
            elif q == 3:
                x = block(5)
            else:
                x = early(q, s)
            for k in range(terms):
                y = acc[k, q] + nt(x, tiles_ref[k, s, q])
                prod[h, k * seg : k * seg + rows, (q % 2) * bsz : (q % 2 + 1) * bsz] = y.astype(BF)

    def mix(n, h):
        return nn(kron[n], prod[h])

    ca = [remote(a_out.at[h], a_in.at[h], as_.at[h], ar.at[h], to_near) for h in range(2)]
    cb = [remote(b_out.at[h], b_in.at[h], bs.at[h], br.at[h], to_far) for h in range(2)]
    cc = [remote(c_out.at[h], c_in.at[h], cs.at[h], cr.at[h], to_near) for h in range(2)]
    for h in range(2):
        late(h)
        a_out[h] = mix(0, h).astype(BF)
        ca[h].start()
        t = mix(1, h)
        ca[h].wait()
        b_out[h] = (t + a_in[h].astype(F32)).astype(BF)
        cb[h].start()
    for h in range(2):
        c_out[h] = mix(2, h).astype(BF)
        cc[h].start()
    loads_in[1].wait()
    loads_in[2].wait()
    for h in range(2):
        own[h] = fo_ref[:, h * half : (h + 1) * half] - mix(3, h)
    for h in range(2):
        cc[h].wait()
        cb[h].wait()
        lanes = slice(h * half, (h + 1) * half)
        res = own[h] - (c_in[h].astype(F32) + b_in[h].astype(F32))
        res_ref[:, lanes] = res
        rb = res.astype(BF)
        for g in range(2):
            q = 2 * h + g
            up = nt(rb[:, g * bsz : (g + 1) * bsz], inv_ref[q])
            at = slice(q * bsz, (q + 1) * bsz)
            upd_ref[:, at] = it_ref[:, at] + RELAXATION * up


def body(iterate, forcing, tiles, inverse_blocks, columns, coupling):
    modes, loads, dofs = iterate.shape
    terms, blocks, slots = tiles.shape[:3]
    bsz = dofs // blocks
    rows = modes * loads
    half = 2 * bsz
    seg = -(-rows // 128) * 128
    shaped = jnp.swapaxes(tiles.reshape(terms, blocks, slots, bsz, bsz), 1, 2)
    inverse = inverse_blocks.reshape(blocks, bsz, bsz)
    out = jax.ShapeDtypeStruct((rows, dofs), F32)
    sem2 = pltpu.SemaphoreType.DMA((2,))
    wire = pltpu.VMEM((2, rows, half), BF)
    vm = pl.BlockSpec(memory_space=pltpu.VMEM)
    flops = 2 * rows * (terms * slots * blocks * bsz * bsz + 4 * terms * seg * dofs)
    upd, res = pl.pallas_call(
        functools.partial(kernel, (modes, loads, bsz, terms, seg)),
        out_shape=(out, out),
        in_specs=[pl.BlockSpec(memory_space=pltpu.SMEM), vm, vm, ANY, ANY, ANY],
        out_specs=(vm, vm),
        scratch_shapes=[
            pltpu.VMEM((rows, dofs), F32),
            pltpu.VMEM((terms, slots, blocks, bsz, bsz), BF),
            pltpu.VMEM((blocks, bsz, bsz), BF),
            pltpu.VMEM((4, rows, half), BF),
            pltpu.VMEM((terms, blocks, rows, bsz), F32),
            pltpu.VMEM((2, terms * seg, half), BF),
            pltpu.VMEM((4, rows, terms * seg), BF),
            pltpu.VMEM((2, rows, half), F32),
            wire, wire, wire, wire, wire, wire,
            pltpu.SemaphoreType.DMA((3,)),
            sem2, sem2, sem2, sem2, sem2, sem2, sem2, sem2,
        ],
        compiler_params=pltpu.CompilerParams(
            collective_id=0, has_side_effects=True, vmem_limit_bytes=44 * 2**20
        ),
        cost_estimate=pl.CostEstimate(flops=flops, bytes_accessed=8 * 2**20, transcendentals=0),
    )(
        columns,
        iterate.reshape(rows, dofs),
        coupling,
        forcing.reshape(rows, dofs),
        shaped,
        inverse,
    )
    shape = (modes, loads, dofs)
    return upd.reshape(shape), res.reshape(shape)


def solution(mesh):
    return jax.shard_map(
        body,
        mesh=mesh,
        in_specs=(
            P("mode", None, "space"),
            P("mode", None, "space"),
            P(None, "space", None, None),
            P("space", None),
            P("space", None),
            P(),
        ),
        out_specs=(P("mode", None, "space"), P("mode", None, "space")),
        check_vma=False,
    )
```

```python
import functools

import jax
import jax.numpy as jnp
from jax import lax
from jax.experimental import pallas as pl
from jax.experimental.pallas import tpu as pltpu
from jax.sharding import PartitionSpec as P

RELAXATION = 0.7
BF = jnp.bfloat16
F32 = jnp.float32
MESH = pl.DeviceIdType.MESH
HBM = pl.BlockSpec(memory_space=pltpu.HBM)


def nt(a, b):
    return lax.dot_general(a, b, (((1,), (1,)), ((), ())), preferred_element_type=F32)


def nn(a, b):
    return jnp.dot(a, b, preferred_element_type=F32)


def iota(shape, dim):
    return lax.broadcasted_iota(jnp.int32, shape, dim)


def unpack(raw, dst, flat, tall, blocks, bsz):
    pairs = bsz // 2
    for t in range(bsz * bsz // 512):
        v = raw[:, t * 512 : (t + 1) * 512].astype(F32)
        for u in range(4):
            at = (4 * t + u) * blocks
            flat[at : at + blocks, :] = v[:, u * 128 : (u + 1) * 128]
    for j in range(blocks):
        a, b, c = [flat[pl.ds(n * blocks + j, pairs, 3 * blocks), :] for n in range(3)]
        turned = pltpu.roll(b, 64, 1)
        low = iota((pairs, 128), 1) < 64
        rolled = pltpu.roll(c, 64, 1)
        tall[0, pl.ds(0, pairs, 2), :] = a
        tall[1, pl.ds(0, pairs, 2), :] = b
        tall[0, pl.ds(1, pairs, 2), :] = jnp.where(low, turned, rolled)
        tall[1, pl.ds(1, pairs, 2), :] = rolled
        dst[j, :, 0:128] = tall[0].astype(BF)
        dst[j, :, 128:bsz] = tall[1][:, : bsz - 128].astype(BF)


def kernel(
    cfg,
    cols_ref, it_hbm, c_hbm, fo_hbm, tiles_hbm, inv_hbm,
    upd_ref, res_ref,
    it_ref, c_ref, fo_ref, tiles_ref, inv_ref, xe, acc, prod, kron, own, a_out, a_in, b_out, b_in, c_out, c_in,
    raw_ref, raw_inv, flat, tall,
    isem, lsem, hs, hr, as_, ar, bs, br, cs, cr,
):
    modes, loads, bsz, terms, seg = cfg
    rows = modes * loads
    half = 2 * bsz
    n_space = lax.axis_size("space")
    me_s = lax.axis_index("space")
    me = lax.axis_index("mode")
    right = lax.rem(me_s + 1, n_space)
    left = lax.rem(me_s + n_space - 1, n_space)
    near = me + 1 - 2 * lax.rem(me, 2)
    far = lax.rem(me + 2, 4)
    diag = lax.rem(near + 2, 4)
    to_right, to_left = (right, me), (left, me)
    to_near, to_far = (me_s, near), (me_s, far)

    barrier = pltpu.get_barrier_semaphore()
    for who in (to_right, to_left, to_near, to_far):
        pl.semaphore_signal(barrier, inc=1, device_id=who, device_id_type=MESH)
    it_in = [
        pltpu.make_async_copy(
            it_hbm.at[:, pl.ds(h * half, half)], it_ref.at[:, pl.ds(h * half, half)], isem.at[h]
        )
        for h in range(2)
    ]
    c_in_ = pltpu.make_async_copy(c_hbm, c_ref, isem.at[2])
    for cp in it_in:
        cp.start()
    c_in_.start()
    loads_in = [
        pltpu.make_async_copy(tiles_hbm, raw_ref, lsem.at[0]),
        pltpu.make_async_copy(fo_hbm, fo_ref, lsem.at[1]),
        pltpu.make_async_copy(inv_hbm, raw_inv, lsem.at[2]),
    ]
    for cp in loads_in:
        cp.start()

    for h in range(2):
        it_in[h].wait()
        xe[1 + h] = it_ref[:, h * half : (h + 1) * half].astype(BF)
    pl.semaphore_wait(barrier, 4)

    def remote(src, dst, s, r, who):
        return pltpu.make_async_remote_copy(
            src_ref=src, dst_ref=dst, send_sem=s, recv_sem=r, device_id=who, device_id_type=MESH
        )

    halo = [
        remote(xe.at[2], xe.at[0], hs.at[0], hr.at[0], to_right),
        remote(xe.at[1], xe.at[3], hs.at[1], hr.at[1], to_left),
    ]
    for cp in halo:
        cp.start()

    c_in_.wait()
    total = c_ref.shape[1]
    col = iota((total, seg), 1)
    pick = (iota((total, seg), 0) == me * modes + col // loads) & (col < rows)
    pick = jnp.where(pick, 1.0, 0.0).astype(BF)
    spread = [nn(c_ref[k].astype(BF), pick).astype(BF) for k in range(terms)]
    same = (iota((rows, seg), 0) % loads) == (iota((rows, seg), 1) % loads)
    for n, dest in enumerate((diag, far, near, me)):
        e = iota((rows, total), 1) == dest * modes + iota((rows, total), 0) // loads
        e = jnp.where(e, 1.0, 0.0).astype(BF)
        for k in range(terms):
            kron[n, :, k * seg : (k + 1) * seg] = jnp.where(same, nn(e, spread[k]), 0.0).astype(BF)
    for h in range(2):
        for k in range(terms):
            prod[h, k * seg + rows : (k + 1) * seg, :] = jnp.zeros((seg - rows, half), BF)

    def block(q):
        p = q + 2
        return xe[p // 2, :, (p % 2) * bsz : (p % 2 + 1) * bsz]

    loads_in[0].wait()

    @pl.loop(0, terms * 3)
    def _(n):
        unpack(raw_ref.at[n // 3, n % 3], tiles_ref.at[n // 3, n % 3], flat, tall, 4, bsz)

    def early(q, s):
        near_, far_ = (q - 1, q - 2) if s == 1 else (q + 1, q + 2)
        return jnp.where(cols_ref[q, s] == near_ + 2, block(near_), block(far_))

    for q in range(4):
        s = 2 if q < 2 else 1
        a0, a1 = block(q), early(q, s)
        for k in range(terms):
            acc[k, q] = nt(a0, tiles_ref[k, 0, q]) + nt(a1, tiles_ref[k, s, q])

    for cp in halo:
        cp.wait()

    def late(h):
        for q in (2 * h, 2 * h + 1):
            s = 1 if q < 2 else 2
            if q == 0:
                x = block(-2)
            elif q == 3:
                x = block(5)
            else:
                x = early(q, s)
            for k in range(terms):
                y = acc[k, q] + nt(x, tiles_ref[k, s, q])
                prod[h, k * seg : k * seg + rows, (q % 2) * bsz : (q % 2 + 1) * bsz] = y.astype(BF)

    def mix(n, h):
        return nn(kron[n], prod[h])

    ca = [remote(a_out.at[h], a_in.at[h], as_.at[h], ar.at[h], to_near) for h in range(2)]
    cb = [remote(b_out.at[h], b_in.at[h], bs.at[h], br.at[h], to_far) for h in range(2)]
    cc = [remote(c_out.at[h], c_in.at[h], cs.at[h], cr.at[h], to_near) for h in range(2)]
    for h in range(2):
        late(h)
        a_out[h] = mix(0, h).astype(BF)
        ca[h].start()
    for h in range(2):
        t = mix(1, h)
        ca[h].wait()
        b_out[h] = (t + a_in[h].astype(F32)).astype(BF)
        cb[h].start()
    for h in range(2):
        c_out[h] = mix(2, h).astype(BF)
        cc[h].start()
    loads_in[1].wait()
    loads_in[2].wait()
    unpack(raw_inv, inv_ref, flat, tall, 4, bsz)
    for h in range(2):
        own[h] = fo_ref[:, h * half : (h + 1) * half] - mix(3, h)
    for h in range(2):
        cc[h].wait()
        cb[h].wait()
        lanes = slice(h * half, (h + 1) * half)
        res = own[h] - (c_in[h].astype(F32) + b_in[h].astype(F32))
        res_ref[:, lanes] = res
        rb = res.astype(BF)
        for g in range(2):
            q = 2 * h + g
            up = nt(rb[:, g * bsz : (g + 1) * bsz], inv_ref[q])
            at = slice(q * bsz, (q + 1) * bsz)
            upd_ref[:, at] = it_ref[:, at] + RELAXATION * up


def body(iterate, forcing, tiles, inverse_blocks, columns, coupling):
    modes, loads, dofs = iterate.shape
    terms, blocks, slots = tiles.shape[:3]
    bsz = dofs // blocks
    rows = modes * loads
    half = 2 * bsz
    seg = -(-rows // 128) * 128
    shaped = jnp.swapaxes(tiles, 1, 2)
    out = jax.ShapeDtypeStruct((rows, dofs), F32)
    sem2 = pltpu.SemaphoreType.DMA((2,))
    wire = pltpu.VMEM((2, rows, half), BF)
    vm = pl.BlockSpec(memory_space=pltpu.VMEM)
    flops = 2 * rows * (terms * slots * blocks * bsz * bsz + 4 * terms * seg * dofs)
    upd, res = pl.pallas_call(
        functools.partial(kernel, (modes, loads, bsz, terms, seg)),
        out_shape=(out, out),
        in_specs=[pl.BlockSpec(memory_space=pltpu.SMEM), HBM, HBM, HBM, HBM, HBM],
        out_specs=(vm, vm),
        scratch_shapes=[
            pltpu.VMEM((rows, dofs), F32),
            pltpu.VMEM(coupling.shape, F32),
            pltpu.VMEM((rows, dofs), F32),
            pltpu.VMEM((terms, slots, blocks, bsz, bsz), BF),
            pltpu.VMEM((blocks, bsz, bsz), BF),
            pltpu.VMEM((4, rows, half), BF),
            pltpu.VMEM((terms, blocks, rows, bsz), F32),
            pltpu.VMEM((2, terms * seg, half), BF),
            pltpu.VMEM((4, rows, terms * seg), BF),
            pltpu.VMEM((2, rows, half), F32),
            wire, wire, wire, wire, wire, wire,
            pltpu.VMEM(tuple(tiles.shape[i] for i in (0, 2, 1, 3)), BF),
            pltpu.VMEM(inverse_blocks.shape, BF),
            pltpu.VMEM((blocks * bsz * bsz // 128, 128), F32),
            pltpu.VMEM((2, bsz, 128), F32),
            pltpu.SemaphoreType.DMA((3,)),
            pltpu.SemaphoreType.DMA((3,)),
            sem2, sem2, sem2, sem2, sem2, sem2, sem2, sem2,
        ],
        compiler_params=pltpu.CompilerParams(
            collective_id=0, has_side_effects=True, vmem_limit_bytes=44 * 2**20
        ),
        cost_estimate=pl.CostEstimate(flops=flops, bytes_accessed=8 * 2**20, transcendentals=0),
    )(
        columns,
        iterate.reshape(rows, dofs),
        coupling,
        forcing.reshape(rows, dofs),
        shaped,
        inverse_blocks,
    )
    shape = (modes, loads, dofs)
    return upd.reshape(shape), res.reshape(shape)


def solution(mesh):
    return jax.shard_map(
        body,
        mesh=mesh,
        in_specs=(
            P("mode", None, "space"),
            P("mode", None, "space"),
            P(None, "space", None, None),
            P("space", None),
            P("space", None),
            P(),
        ),
        out_specs=(P("mode", None, "space"), P("mode", None, "space")),
        check_vma=False,
    )
```
